1024 devices in a mesh: blk: 64 (over y, z_lo), slab: 16 (over x, z_hi, core).
Axes of the slice: x: 4, y: 4, z: 32 (z_hi: 2, z_lo: 16; z = z_hi * 16 + z_lo), core: 2. Of those that a mesh axis runs over, the one named last changes fastest.
Arguments:
- photo_features: bfloat16 [262144, 1152], P(('blk', 'slab')), may hold values from -1 to 1
- text_features: bfloat16 [262144, 1152], P(('blk', 'slab')), may hold values from -1 to 1
- partner_displacement: int32 [64, 16], replicated, may hold values from 0 to 255
- multiplier_factor: float32 [], replicated, may hold values from 1 to 4
- additive_shift_term: float32 [], replicated, may hold values from -3 to -1
Outputs:
- photo_feature_derivative: float32 [262144, 1152], P(('blk', 'slab'))
- text_feature_derivative: float32 [262144, 1152], P(('blk', 'slab'))
The draws below stay inside these ranges and needn't reach their ends.
All inputs are finite; a program needn't handle non-finite values.
Results may differ from the reference program's by a relative error of at most 0.0025.
Values may be sent and summed in bfloat16 or wider, within the bound.
A program may use at most 32 MiB of HBM per device.

```python
import math
import jax
import jax.numpy as jnp
from jax import lax

FEATURE_DIM = 1152
MATCHES_IN_GROUP = 256
STEPS = 4
BATCH = 262144
N_BLK = 64
N_SLAB = 16


def set_ends(entries, rng, least, largest):
    longest = entries.shape.index(max(entries.shape))
    spots = []
    for shift in (0, 1):
        where = [jax.random.randint(jax.random.fold_in(rng, axis), (), 0, length) for axis, length in enumerate(entries.shape)]
        where[longest] = (where[longest] + shift) % entries.shape[longest]
        spots.append(tuple(where))
    return entries.at[spots[0]].set(least).at[spots[1]].set(largest)


def block_levels(rng, extent, split, least, top_value):
    loudness, own = 1.0, jax.random.fold_in(rng, 6)
    for dim, shards_of in split:
        heights = jnp.exp(jax.random.uniform(jax.random.fold_in(own, dim), (shards_of,), jnp.float32, least / len(split), top_value / len(split)))
        loudness = loudness * jnp.repeat(heights, extent[dim] // shards_of).reshape([-1 if axis == dim else 1 for axis in range(len(extent))])
    return loudness


def scatter_about(stream_key, extent, deviation, most, pieces=(), kind=jnp.bfloat16):
    array = deviation * jax.random.normal(stream_key, extent, jnp.float32)
    if pieces:
        array = array * block_levels(stream_key, extent, pieces, -0.22, 0.18)
    return jnp.clip(array, -most, most).astype(kind)


def setup_inputs(seed: int = 0) -> dict:
    arg_keys = jax.random.split(jax.random.key(seed), 6)
    return {
        "photo_features": scatter_about(arg_keys[0], (BATCH, FEATURE_DIM), 0.17, 1.0, ((0, 1024),)),
        "text_features": scatter_about(arg_keys[1], (BATCH, FEATURE_DIM), 0.17, 1.0, ((0, 1024),)),
        "partner_displacement": set_ends(jax.random.randint(arg_keys[2], (N_BLK, N_SLAB), 0, MATCHES_IN_GROUP), jax.random.fold_in(arg_keys[2], 1), 0, MATCHES_IN_GROUP - 1).astype(jnp.int32),
        "multiplier_factor": jnp.clip(jnp.exp(jax.random.uniform(arg_keys[3], (), jnp.float32, math.log(1.0), math.log(4.0))), 1.0, 4.0),
        "additive_shift_term": jnp.clip(jax.random.uniform(arg_keys[4], (), jnp.float32, -3.0, -1.0), -3.0, -1.0),
    }


def reference(photo_features, text_features, partner_displacement, multiplier_factor, additive_shift_term):
    image_grid = photo_features.reshape(N_BLK, N_SLAB, MATCHES_IN_GROUP, FEATURE_DIM)
    caption_grid = text_features.reshape(N_BLK, N_SLAB, MATCHES_IN_GROUP, FEATURE_DIM)
    row_ids = jnp.arange(MATCHES_IN_GROUP, dtype=jnp.int32)[:, None]
    col_ids = jnp.arange(MATCHES_IN_GROUP, dtype=jnp.int32)[None, :]

    def one_block(b, grads):
        photo_increment, text_increment = grads
        photo_group_available = lax.dynamic_index_in_dim(image_grid, b, 0, False).astype(jnp.float32)
        offset_now = lax.dynamic_index_in_dim(partner_displacement, b, 0, False)
        photo_derivative_total = jnp.zeros((N_SLAB, MATCHES_IN_GROUP, FEATURE_DIM), jnp.float32)
        for k in range(STEPS):
            source = ((b - k) % N_BLK).astype(jnp.int32)
            block_now = lax.dynamic_index_in_dim(caption_grid, source, 0, False)
            text_group_available = jnp.roll(block_now, 1, axis=0).astype(jnp.float32)
            similarity_matrix = multiplier_factor * jnp.einsum('kce,kle->kcl', photo_group_available, text_group_available) + additive_shift_term
            likely = jax.nn.sigmoid(similarity_matrix)
            if k == 0:
                target = (col_ids[None] == (row_ids[None] + offset_now[:, None, None]) % MATCHES_IN_GROUP).astype(jnp.float32)
                likely = likely - target
            rounded = lax.optimization_barrier(likely.astype(jnp.bfloat16))
            weight = rounded.astype(jnp.float32)
            photo_derivative_total = photo_derivative_total + jnp.einsum('src,scd->srd', weight, text_group_available)
            caption_part = jnp.roll(jnp.einsum('src,srd->scd', weight, photo_group_available), -1, axis=0)
            previous = lax.dynamic_index_in_dim(text_increment, source, 0, False)
            text_increment = lax.dynamic_update_index_in_dim(text_increment, previous + caption_part, source, 0)
        photo_increment = lax.dynamic_update_index_in_dim(photo_increment, photo_derivative_total, b, 0)
        return (photo_increment, text_increment)

    empty = jnp.zeros((N_BLK, N_SLAB, MATCHES_IN_GROUP, FEATURE_DIM), jnp.float32)
    photo_increment, text_increment = lax.fori_loop(0, N_BLK, one_block, (empty, empty))
    photo_feature_derivative = (multiplier_factor * photo_increment).reshape(MATCHES_IN_GROUP * N_BLK * N_SLAB, FEATURE_DIM)
    text_feature_derivative = (multiplier_factor * text_increment).reshape(MATCHES_IN_GROUP * N_BLK * N_SLAB, FEATURE_DIM)
    return (photo_feature_derivative, text_feature_derivative)
```

```python
import functools

import jax
import jax.numpy as jnp
from jax import lax
from jax.experimental import pallas as pl
from jax.experimental.pallas import tpu as pltpu
from jax.sharding import PartitionSpec as P

MESH = pl.DeviceIdType.MESH
STEPS = 4
NX, NY, HALF = 4, 4, 16
RING = 2 * HALF
X0 = HALF - 1
K0 = HALF + STEPS - 1
SLOTS = K0 + STEPS
PARTS = 2


def device(x, y, z, core):
    x, y, z = (x + NX) % NX, (y + NY) % NY, (z + RING) % RING
    return {"blk": y * HALF + z % HALF, "slab": x * 4 + (z // HALF) * 2 + core}


def kernel(
    photo, text, shifts, factor, bias, photo_out, text_out,
    own, slots, totals, ring_send, ring_recv, near_send, near_recv, side_send, side_recv, first_send, local,
):
    blk, slab = lax.axis_index("blk"), lax.axis_index("slab")
    x, half, core = slab // 4, (slab // 2) % 2, slab % 2
    y, z_lo = blk // HALF, blk % HALF
    z = half * HALF + z_lo
    other = 1 - core
    s = 2 * core - 1
    u = jnp.where(core == 1, z_lo, HALF - 1 - z_lo)
    rows = own.shape[1]
    piece = rows // PARTS

    @pl.when(core == 0)
    def _():
        pltpu.make_async_copy(text, own.at[0], local.at[0]).start()
        pltpu.make_async_copy(photo, own.at[1], local.at[1]).start()

    @pl.when(core == 1)
    def _():
        pltpu.make_async_copy(photo, own.at[0], local.at[0]).start()
        pltpu.make_async_copy(text, own.at[1], local.at[1]).start()

    ahead = device(x, y, z + s, core)
    behind = device(x, y, z - s, core)
    partner = device(x, y, z, other)
    x_far = jnp.where(core == 0, x - (1 - half), x + half)

    def x_from(z_source):
        h = ((z_source + RING) % RING) // HALF
        return jnp.where(core == 0, x - h, x + (1 - h))

    inject = device(x_far, y, z - s, other)
    inject_from = device(x_from(z - s), y, z - s, other)
    around = device(x, y - s, half * HALF + (z_lo + s * (HALF - 3) + RING) % HALF, other)
    k_side = jnp.minimum(HALF - u, STEPS - 1)
    side = device(x_far, y + s, z + s * k_side, other)

    barrier = pltpu.get_barrier_semaphore()

    def greet(d):
        pl.semaphore_signal(barrier, inc=1, device_id=d, device_id_type=MESH)

    for d in (ahead, behind, partner, inject, inject_from):
        greet(d)

    @pl.when(u <= 2)
    def _():
        greet(around)

    @pl.when(u >= HALF - 3)
    def _():
        greet(side)

    @pl.when(u == HALF - 1)
    def _():
        for k in range(1, STEPS):
            greet(device(x_from(z + s * k), y + s, z + s * k, other))

    peers = 5 + jnp.where(u <= 2, 1, 0) + jnp.where(u >= HALF - 3, 1, 0) + jnp.where(u == HALF - 1, 3, 0)
    pl.semaphore_wait(barrier, peers)

    def remote(src, dst, send, recv, d):
        return pltpu.make_async_remote_copy(
            src_ref=src, dst_ref=dst, send_sem=send, recv_sem=recv, device_id=d, device_id_type=MESH
        )

    pltpu.make_async_copy(text, own.at[1], local.at[1]).wait()

    def part(ref, slot, q):
        return ref.at[slot, pl.ds(pl.multiple_of(q * piece, piece), piece)]

    def injected(q):
        return remote(part(own, 1, q), part(slots, 0, q), ring_send.at[X0, q], ring_recv.at[0, q], inject)

    def onward(j, q):
        return remote(part(slots, j, q), part(slots, j + 1, q), ring_send.at[j, q], ring_recv.at[j + 1, q], ahead)

    for q in range(PARTS):
        injected(q).start()

    pltpu.make_async_copy(text, own.at[0], local.at[0]).wait()
    to_partner = remote(own.at[0], slots.at[K0], first_send.at[0], near_recv.at[0], partner)
    to_around = remote(own.at[0], slots.at[K0 + 3], first_send.at[1], near_recv.at[3], around)
    to_side = remote(own.at[1], slots.at[X0 + k_side], first_send.at[2], side_recv.at[k_side], side)
    to_partner.start()
    is_around, is_side = u <= 2, u >= HALF - 3
    pl.when(is_around)(to_around.start)
    pl.when(is_side)(to_side.start)

    def near_on(k):
        return remote(slots.at[K0 + k], slots.at[K0 + k + 1], near_send.at[k], near_recv.at[k + 1], ahead)

    def near_back(k):
        return remote(slots.at[K0 + k], slots.at[K0 + k - 1], near_send.at[k], near_recv.at[k - 1], behind)

    def side_back(k):
        return remote(slots.at[X0 + k], slots.at[X0 + k + 1], side_send.at[k], side_recv.at[k + 1], behind)

    def near_arrived(k):
        remote(slots.at[K0 + k], slots.at[K0 + k], near_send.at[k], near_recv.at[k], ahead).wait_recv()

    def goes_on(k):
        return (u >= k) & (u < HALF - 1)

    def goes_back(k):
        return (u < k) & (u >= 1)

    def near_plain(k):
        @pl.when(u >= k)
        def _():
            near_arrived(k)

        pl.when(goes_on(k))(near_on(k).start)

    def near_last():
        near_arrived(3)
        pl.when(goes_back(3))(near_back(3).start)

    def near_wrapped(k):
        @pl.when(u < k)
        def _():
            near_arrived(k)

        if k == 2:
            pl.when(goes_back(k))(near_back(k).start)

    def side_goes(k):
        return u >= HALF - 3 + (3 - k)

    def side_step(k):
        @pl.when(side_goes(k))
        def _():
            remote(slots.at[X0 + k], slots.at[X0 + k], side_send.at[k], side_recv.at[k], ahead).wait_recv()

        if k < 3:
            pl.when(side_goes(k))(side_back(k).start)

    def ring_step(j):
        for q in range(PARTS):
            remote(part(slots, j, q), part(slots, j, q), ring_send.at[j, q], ring_recv.at[j, q], ahead).wait_recv()
            onward(j, q).start()

    def ring_steps(first, last):
        def step(j, carry):
            ring_step(j)
            return carry

        lax.fori_loop(first, last, step, 0)

    multiplier, shift = factor[0], bias[0]
    caption_side = lax.rem(slab + 1, 16)
    as_image = shifts[blk, slab]
    as_caption = rows - shifts[blk, caption_side]
    near_offset = jnp.where(core == 0, as_caption, as_image)
    far_offset = jnp.where(core == 0, as_image, as_caption)
    position = lax.broadcasted_iota(jnp.int32, (rows, rows), 0)
    column = lax.broadcasted_iota(jnp.int32, (rows, rows), 1)

    def task(role, k, slot, offset):
        block = slots[slot]
        similarity = multiplier * lax.dot_general(
            own[role], block, (((1,), (1,)), ((), ())), preferred_element_type=jnp.float32
        ) + shift
        likely = jax.nn.sigmoid(similarity)
        hit = jnp.where(column == lax.rem(position + offset, rows), 1.0, 0.0)
        likely = likely - hit * jnp.where(k == 0, 1.0, 0.0)
        weight = likely.astype(jnp.bfloat16)
        totals[role] += jnp.dot(weight, block, preferred_element_type=jnp.float32)

    def near_task(k):
        task(0, k, K0 + k, near_offset)

    def far_task(k):
        task(1, k, jnp.where(u + k < HALF, X0 - k, X0 + k), far_offset)

    totals[...] = jnp.zeros_like(totals)
    near_plain(0)
    ring_steps(0, 2)
    near_plain(1)
    ring_steps(2, 4)
    near_plain(2)
    ring_steps(4, 6)
    near_last()
    side_step(1)
    ring_steps(6, 7)
    near_wrapped(2)
    side_step(2)
    ring_steps(7, 8)
    near_wrapped(1)
    side_step(3)

    def near_loop(k, carry):
        ring_step(HALF // 2 + k)
        near_task(k)
        return carry

    lax.fori_loop(0, STEPS, near_loop, 0)

    @pl.when(core == 0)
    def _():
        pltpu.make_async_copy(totals.at[0], text_out, local.at[0]).start()

    @pl.when(core == 1)
    def _():
        pltpu.make_async_copy(totals.at[0], photo_out, local.at[0]).start()

    def far_loop(k, carry):
        j = X0 - 3 + k

        @pl.when(k < STEPS - 1)
        def _():
            ring_step(j)

        @pl.when(k == STEPS - 1)
        def _():
            for q in range(PARTS):
                remote(part(slots, X0, q), part(slots, X0, q), ring_send.at[X0, q], ring_recv.at[X0, q], ahead).wait_recv()

        far_task(STEPS - 1 - k)
        return carry

    lax.fori_loop(0, STEPS, far_loop, 0)

    @pl.when(core == 0)
    def _():
        pltpu.make_async_copy(totals.at[1], photo_out, local.at[1]).start()

    @pl.when(core == 1)
    def _():
        pltpu.make_async_copy(totals.at[1], text_out, local.at[1]).start()

    def sent(j, carry):
        for q in range(PARTS):
            onward(j, q).wait_send()
        return carry

    lax.fori_loop(0, X0, sent, 0)
    for q in range(PARTS):
        injected(q).wait_send()
    to_partner.wait_send()
    pl.when(is_around)(to_around.wait_send)
    pl.when(is_side)(to_side.wait_send)
    for k in range(3):
        pl.when(goes_on(k))(near_on(k).wait_send)
    for k in (2, 3):
        pl.when(goes_back(k))(near_back(k).wait_send)
    for k in (1, 2):
        pl.when(side_goes(k))(side_back(k).wait_send)
    for role in range(2):
        pltpu.make_async_copy(totals.at[role], photo_out, local.at[role]).wait()


def body(photo_features, text_features, partner_displacement, multiplier_factor, additive_shift_term):
    rows, width = photo_features.shape
    anywhere = pl.BlockSpec(memory_space=pl.ANY)
    scalars = pl.BlockSpec(memory_space=pltpu.SMEM)
    total = jax.ShapeDtypeStruct((rows, width), jnp.float32)
    photo, text = pl.pallas_call(
        kernel,
        out_shape=(total, total),
        in_specs=[anywhere, anywhere, scalars, scalars, scalars],
        out_specs=(anywhere, anywhere),
        scratch_shapes=[
            pltpu.VMEM((2, rows, width), jnp.bfloat16),
            pltpu.VMEM((SLOTS, rows, width), jnp.bfloat16),
            pltpu.VMEM((2, rows, width), jnp.float32),
            pltpu.SemaphoreType.DMA((HALF, PARTS)),
            pltpu.SemaphoreType.DMA((HALF, PARTS)),
            pltpu.SemaphoreType.DMA((STEPS,)),
            pltpu.SemaphoreType.DMA((STEPS,)),
            pltpu.SemaphoreType.DMA((STEPS,)),
            pltpu.SemaphoreType.DMA((STEPS,)),
            pltpu.SemaphoreType.DMA((3,)),
            pltpu.SemaphoreType.DMA((2,)),
        ],
        compiler_params=pltpu.CompilerParams(
            collective_id=0, has_side_effects=True, vmem_limit_bytes=40 * 2**20
        ),
        cost_estimate=pl.CostEstimate(
            flops=32 * rows * rows * width, bytes_accessed=12 * rows * width, transcendentals=8 * rows * rows
        ),
    )(
        photo_features, text_features, partner_displacement,
        multiplier_factor.reshape(1), additive_shift_term.reshape(1),
    )
    return multiplier_factor * photo, multiplier_factor * text


def solution(mesh):
    return jax.shard_map(
        body,
        mesh=mesh,
        in_specs=(P(("blk", "slab"), None), P(("blk", "slab"), None), P(), P(), P()),
        out_specs=(P(("blk", "slab"), None), P(("blk", "slab"), None)),
        check_vma=False,
    )
```

```python
import functools

import jax
import jax.numpy as jnp
from jax import lax
from jax.experimental import pallas as pl
from jax.experimental.pallas import tpu as pltpu
from jax.sharding import PartitionSpec as P

MESH = pl.DeviceIdType.MESH
STEPS = 4
NX, NY, HALF = 4, 4, 16
RING = 2 * HALF
X0 = HALF - 1
K0 = HALF + STEPS - 1
SLOTS = K0 + STEPS
LAST = HALF - 1
PARTS = 4


def device(x, y, z, core):
    x, y, z = (x + NX) % NX, (y + NY) % NY, (z + RING) % RING
    return {"blk": y * HALF + z % HALF, "slab": x * 4 + (z // HALF) * 2 + core}


def kernel(
    photo, text, shifts, factor, bias, photo_out, text_out,
    own, slots, totals, sums, shift_rows, ring_send, ring_recv, near_send, near_recv, side_send, side_recv, first_send,
    own_send, own_recv, sum_send, sum_recv, local,
):
    blk, slab = lax.axis_index("blk"), lax.axis_index("slab")
    x, half, core = slab // 4, (slab // 2) % 2, slab % 2
    y, z_lo = blk // HALF, blk % HALF
    z = half * HALF + z_lo
    other = 1 - core
    s = 2 * core - 1
    u = jnp.where(core == 1, z_lo, HALF - 1 - z_lo)
    rows = own.shape[1]
    piece = rows // PARTS

    pltpu.make_async_copy(shifts, shift_rows, local.at[2]).start()

    @pl.when(core == 0)
    def _():
        pltpu.make_async_copy(text, own.at[0], local.at[0]).start()
        pltpu.make_async_copy(photo, own.at[1], local.at[1]).start()

    @pl.when(core == 1)
    def _():
        pltpu.make_async_copy(photo, own.at[0], local.at[0]).start()
        pltpu.make_async_copy(text, own.at[1], local.at[1]).start()

    ahead = device(x, y, z + s, core)
    behind = device(x, y, z - s, core)
    partner = device(x, y, z, other)
    x_far = jnp.where(core == 0, x - (1 - half), x + half)

    def x_from(z_source):
        h = ((z_source + RING) % RING) // HALF
        return jnp.where(core == 0, x - h, x + (1 - h))

    inject = device(x_far, y, z - s, other)
    inject_from = device(x_from(z - s), y, z - s, other)
    around = device(x, y - s, half * HALF + (z_lo + s * (HALF - 3) + RING) % HALF, other)
    k_side = jnp.minimum(HALF - u, STEPS - 1)
    side = device(x_far, y + s, z + s * k_side, other)

    barrier = pltpu.get_barrier_semaphore()

    def greet(d):
        pl.semaphore_signal(barrier, inc=1, device_id=d, device_id_type=MESH)

    for d in (ahead, behind, partner, inject, inject_from):
        greet(d)

    @pl.when(u <= 2)
    def _():
        greet(around)

    @pl.when(u >= HALF - 3)
    def _():
        greet(side)

    @pl.when(u == HALF - 1)
    def _():
        for k in range(1, STEPS):
            greet(device(x_from(z + s * k), y + s, z + s * k, other))

    peers = 5 + jnp.where(u <= 2, 1, 0) + jnp.where(u >= HALF - 3, 1, 0) + jnp.where(u == HALF - 1, 3, 0)
    pl.semaphore_wait(barrier, peers)

    def remote(src, dst, send, recv, d):
        return pltpu.make_async_remote_copy(
            src_ref=src, dst_ref=dst, send_sem=send, recv_sem=recv, device_id=d, device_id_type=MESH
        )

    pltpu.make_async_copy(text, own.at[1], local.at[1]).wait()

    def part(ref, slot, q):
        return ref.at[slot, pl.ds(pl.multiple_of(q * piece, piece), piece)]

    def injected(q):
        return remote(part(own, 1, q), part(slots, 0, q), ring_send.at[X0, q], ring_recv.at[0, q], inject)

    def onward(j, q):
        return remote(part(slots, j, q), part(slots, j + 1, q), ring_send.at[j, q], ring_recv.at[j + 1, q], ahead)

    for q in range(PARTS):
        injected(q).start()

    pltpu.make_async_copy(text, own.at[0], local.at[0]).wait()
    to_partner = remote(own.at[0], slots.at[K0], first_send.at[0], near_recv.at[0], partner)
    to_around = remote(own.at[0], slots.at[K0 + 3], first_send.at[1], near_recv.at[3], around)
    to_side = remote(own.at[1], slots.at[X0 + k_side], first_send.at[2], side_recv.at[k_side], side)
    to_partner.start()
    is_around, is_side = u <= 2, u >= HALF - 3
    pl.when(is_around)(to_around.start)
    pl.when(is_side)(to_side.start)

    def near_on(k):
        return remote(slots.at[K0 + k], slots.at[K0 + k + 1], near_send.at[k], near_recv.at[k + 1], ahead)

    def near_back(k):
        return remote(slots.at[K0 + k], slots.at[K0 + k - 1], near_send.at[k], near_recv.at[k - 1], behind)

    def side_back(k):
        return remote(slots.at[X0 + k], slots.at[X0 + k + 1], side_send.at[k], side_recv.at[k + 1], behind)

    def near_arrived(k):
        remote(slots.at[K0 + k], slots.at[K0 + k], near_send.at[k], near_recv.at[k], ahead).wait_recv()

    def goes_on(k):
        return (u >= k) & (u < LAST - 2)

    def takes_blocks(k):
        return (u >= k) & (u < LAST - 1) if k else u >= 0

    def lends(k):
        return (u == 2) | (u == 1) if k == 1 else u == 2

    def lend(k):
        place = jnp.where(u == 2, 1 + k, 3)
        return remote(slots.at[K0 + k], own.at[place], own_send.at[k], own_recv.at[place], partner)

    def sum_on(n):
        return remote(sums.at[n], sums.at[2 + n], sum_send.at[n], sum_recv.at[n], ahead)

    def own_arrived(place):
        remote(own.at[place], own.at[place], own_send.at[1], own_recv.at[place], partner).wait_recv()

    def sum_arrived(n):
        remote(sums.at[2 + n], sums.at[2 + n], sum_send.at[n], sum_recv.at[n], ahead).wait_recv()

    def goes_back(k):
        return (u < k) & (u >= 1)

    def near_plain(k):
        @pl.when(takes_blocks(k))
        def _():
            near_arrived(k)

        if k < 3:
            pl.when(goes_on(k))(near_on(k).start)
        if k in (1, 2):
            pl.when(lends(k))(lend(k).start)

    def near_direct():
        @pl.when(u < 3)
        def _():
            near_arrived(3)

        pl.when(goes_back(3))(near_back(3).start)

    def near_wrapped(k):
        @pl.when(u < k)
        def _():
            near_arrived(k)

        if k == 2:
            pl.when(goes_back(k))(near_back(k).start)

    def side_goes(k):
        return u >= HALF - 3 + (3 - k)

    def side_step(k):
        @pl.when(side_goes(k))
        def _():
            remote(slots.at[X0 + k], slots.at[X0 + k], side_send.at[k], side_recv.at[k], ahead).wait_recv()

        if k < 3:
            pl.when(side_goes(k))(side_back(k).start)

    def ring_step(j):
        for q in range(PARTS):
            remote(part(slots, j, q), part(slots, j, q), ring_send.at[j, q], ring_recv.at[j, q], ahead).wait_recv()
            onward(j, q).start()

    pltpu.make_async_copy(shifts, shift_rows, local.at[2]).wait()
    multiplier, shift = factor[0], bias[0]
    at_blk = lax.broadcasted_iota(jnp.int32, (1, shift_rows.shape[1]), 1) == blk

    def shift_of(slab_index):
        return jnp.sum(jnp.where(at_blk, shift_rows[pl.ds(slab_index, 1), :], 0), axis=1, keepdims=True)

    as_image = shift_of(slab)
    as_caption = rows - shift_of(lax.rem(slab + 1, 16))
    near_offset = jnp.where(core == 0, as_caption, as_image)
    far_offset = jnp.where(core == 0, as_image, as_caption)

    def task(role, k, block, offset, first=0):
        similarity = multiplier * lax.dot_general(
            own[role], block, (((1,), (1,)), ((), ())), preferred_element_type=jnp.float32
        ) + shift
        likely = jax.nn.sigmoid(similarity)
        position = lax.broadcasted_iota(jnp.int32, likely.shape, 0)
        column = lax.broadcasted_iota(jnp.int32, likely.shape, 1) + first
        hit = jnp.where(column == lax.rem(position + offset, rows), 1.0, 0.0)
        likely = likely - hit * jnp.where(k == 0, 1.0, 0.0)
        weight = likely.astype(jnp.bfloat16)
        totals[role] += jnp.dot(weight, block, preferred_element_type=jnp.float32)

    totals[...] = jnp.zeros_like(totals)

    def step(j, carry):
        ring_step(j)

        for first, action in (
            (1, lambda: near_plain(0)),
            (3, lambda: near_plain(1)),
            (4, near_direct),
            (4, lambda: side_step(1)),
            (5, lambda: near_plain(2)),
            (7, lambda: near_wrapped(2)),
            (7, lambda: side_step(2)),
            (8, lambda: near_plain(3)),
            (10, lambda: near_wrapped(1)),
            (10, lambda: side_step(3)),
        ):
            pl.when(j == first)(action)

        @pl.when((u == LAST - 2) & (j >= 5) & (j <= 7))
        def _():
            pl.when(j == 5)(lambda: own_arrived(2))
            pl.when(j == 7)(lambda: own_arrived(3))

            for n in range(2):
                @pl.when((j != 6) | (n == 0))
                def _():
                    task(jnp.where(j == 7, 3, 2), 1, slots[K0 + jnp.where(j == 6, 2, n)], near_offset)

            for n in range(2):
                @pl.when(j == 6 + n)
                def _():
                    sums[n] = totals[2 + n].astype(jnp.bfloat16)
                    sum_on(n).start()

        @pl.when((u == LAST - 1) & (j == 10))
        def _():
            own_arrived(3)
            task(3, 1, slots[K0], near_offset)
            sum_arrived(1)
            sums[1] = (totals[3] + sums[3].astype(jnp.float32)).astype(jnp.bfloat16)
            sum_on(1).start()
            sum_arrived(0)
            totals[0] += sums[2].astype(jnp.float32)

        @pl.when((j == 8) | ((j >= 9) & (j <= 11) & (u < LAST - 1)))
        def _():
            k = jnp.where(j == 8, 0, jnp.where(j == 9, 2, jnp.where(j == 10, 3, 1)))
            task(0, k, slots[K0 + k], near_offset)

        @pl.when((u == LAST) & (j == 13))
        def _():
            sum_arrived(1)
            totals[0] += sums[3].astype(jnp.float32)

        @pl.when((j == 13) & (core == 0))
        def _():
            pltpu.make_async_copy(totals.at[0], text_out, local.at[0]).start()

        @pl.when((j == 13) & (core == 1))
        def _():
            pltpu.make_async_copy(totals.at[0], photo_out, local.at[0]).start()

        @pl.when(j >= X0 - 3)
        def _():
            k = X0 - j
            task(1, k, slots[jnp.where(u + k < HALF, X0 - k, X0 + k)], far_offset)

        return carry

    lax.fori_loop(0, X0, step, 0)
    for q in range(PARTS):
        last = part(slots, X0, q)
        remote(last, last, ring_send.at[X0, q], ring_recv.at[X0, q], ahead).wait_recv()
        task(1, 0, slots[X0, q * piece : (q + 1) * piece], far_offset, q * piece)

    @pl.when(core == 0)
    def _():
        pltpu.make_async_copy(totals.at[1], photo_out, local.at[1]).start()

    @pl.when(core == 1)
    def _():
        pltpu.make_async_copy(totals.at[1], text_out, local.at[1]).start()

    def sent(j, carry):
        for q in range(PARTS):
            onward(j, q).wait_send()
        return carry

    lax.fori_loop(0, X0, sent, 0)
    for q in range(PARTS):
        injected(q).wait_send()
    to_partner.wait_send()
    pl.when(is_around)(to_around.wait_send)
    pl.when(is_side)(to_side.wait_send)
    for k in range(3):
        pl.when(goes_on(k))(near_on(k).wait_send)
    for k in (2, 3):
        pl.when(goes_back(k))(near_back(k).wait_send)
    for k in (1, 2):
        pl.when(side_goes(k))(side_back(k).wait_send)
    for k in (1, 2):
        pl.when(lends(k))(lend(k).wait_send)
    pl.when(u == LAST - 2)(sum_on(0).wait_send)
    pl.when((u == LAST - 2) | (u == LAST - 1))(sum_on(1).wait_send)
    for role in range(2):
        pltpu.make_async_copy(totals.at[role], photo_out, local.at[role]).wait()


def body(photo_features, text_features, partner_displacement, multiplier_factor, additive_shift_term):
    rows, width = photo_features.shape
    anywhere = pl.BlockSpec(memory_space=pl.ANY)
    hbm = pl.BlockSpec(memory_space=pltpu.HBM)
    scalars = pl.BlockSpec(memory_space=pltpu.SMEM)
    total = jax.ShapeDtypeStruct((rows, width), jnp.float32)
    photo, text = pl.pallas_call(
        kernel,
        out_shape=(total, total),
        in_specs=[hbm, hbm, hbm, scalars, scalars],
        out_specs=(anywhere, anywhere),
        scratch_shapes=[
            pltpu.VMEM((4, rows, width), jnp.bfloat16),
            pltpu.VMEM((SLOTS, rows, width), jnp.bfloat16),
            pltpu.VMEM((4, rows, width), jnp.float32),
            pltpu.VMEM((4, rows, width), jnp.bfloat16),
            pltpu.VMEM(partner_displacement.shape[::-1], jnp.int32),
            pltpu.SemaphoreType.DMA((HALF, PARTS)),
            pltpu.SemaphoreType.DMA((HALF, PARTS)),
            pltpu.SemaphoreType.DMA((STEPS,)),
            pltpu.SemaphoreType.DMA((STEPS,)),
            pltpu.SemaphoreType.DMA((STEPS,)),
            pltpu.SemaphoreType.DMA((STEPS,)),
            pltpu.SemaphoreType.DMA((3,)),
            pltpu.SemaphoreType.DMA((STEPS,)),
            pltpu.SemaphoreType.DMA((STEPS,)),
            pltpu.SemaphoreType.DMA((2,)),
            pltpu.SemaphoreType.DMA((2,)),
            pltpu.SemaphoreType.DMA((3,)),
        ],
        compiler_params=pltpu.CompilerParams(
            collective_id=0, has_side_effects=True, vmem_limit_bytes=40 * 2**20
        ),
        cost_estimate=pl.CostEstimate(
            flops=32 * rows * rows * width, bytes_accessed=12 * rows * width, transcendentals=8 * rows * rows
        ),
    )(
        photo_features, text_features, partner_displacement.T,
        multiplier_factor.reshape(1), additive_shift_term.reshape(1),
    )
    return multiplier_factor * photo, multiplier_factor * text


def solution(mesh):
    return jax.shard_map(
        body,
        mesh=mesh,
        in_specs=(P(("blk", "slab"), None), P(("blk", "slab"), None), P(), P(), P()),
        out_specs=(P(("blk", "slab"), None), P(("blk", "slab"), None)),
        check_vma=False,
    )
```

```python
import functools

import jax
import jax.numpy as jnp
from jax import lax
from jax.experimental import pallas as pl
from jax.experimental.pallas import tpu as pltpu
from jax.sharding import PartitionSpec as P

MESH = pl.DeviceIdType.MESH
STEPS = 4
NX, NY, HALF = 4, 4, 16
RING = 2 * HALF
X0 = HALF - 1
K0 = HALF + STEPS - 1
SLOTS = K0 + STEPS
LAST = HALF - 1
PARTS = 4


def device(x, y, z, core):
    x, y, z = (x + NX) % NX, (y + NY) % NY, (z + RING) % RING
    return {"blk": y * HALF + z % HALF, "slab": x * 4 + (z // HALF) * 2 + core}


def kernel(
    photo, text, shifts, factor, bias, photo_out, text_out,
    own, slots, totals, sums, shift_rows, ring_send, ring_recv, near_send, near_recv, side_send, side_recv, first_send,
    own_send, own_recv, sum_send, sum_recv, local,
):
    blk, slab = lax.axis_index("blk"), lax.axis_index("slab")
    x, half, core = slab // 4, (slab // 2) % 2, slab % 2
    y, z_lo = blk // HALF, blk % HALF
    z = half * HALF + z_lo
    other = 1 - core
    s = 2 * core - 1
    u = jnp.where(core == 1, z_lo, HALF - 1 - z_lo)
    rows = own.shape[1]
    piece = rows // PARTS

    pltpu.make_async_copy(shifts, shift_rows, local.at[2]).start()

    @pl.when(core == 0)
    def _():
        pltpu.make_async_copy(text, own.at[0], local.at[0]).start()
        pltpu.make_async_copy(photo, own.at[1], local.at[1]).start()

    @pl.when(core == 1)
    def _():
        pltpu.make_async_copy(photo, own.at[0], local.at[0]).start()
        pltpu.make_async_copy(text, own.at[1], local.at[1]).start()

    ahead = device(x, y, z + s, core)
    behind = device(x, y, z - s, core)
    partner = device(x, y, z, other)
    x_far = jnp.where(core == 0, x - (1 - half), x + half)

    def x_from(z_source):
        h = ((z_source + RING) % RING) // HALF
        return jnp.where(core == 0, x - h, x + (1 - h))

    inject = device(x_far, y, z - s, other)
    inject_from = device(x_from(z - s), y, z - s, other)
    around = device(x, y - s, half * HALF + (z_lo + s * (HALF - 3) + RING) % HALF, other)
    k_side = jnp.minimum(HALF - u, STEPS - 1)
    side = device(x_far, y + s, z + s * k_side, other)

    barrier = pltpu.get_barrier_semaphore()

    def greet(d):
        pl.semaphore_signal(barrier, inc=1, device_id=d, device_id_type=MESH)

    for d in (ahead, behind, partner, inject, inject_from):
        greet(d)

    @pl.when(u <= 2)
    def _():
        greet(around)

    @pl.when(u >= HALF - 3)
    def _():
        greet(side)

    @pl.when(u == HALF - 1)
    def _():
        for k in range(1, STEPS):
            greet(device(x_from(z + s * k), y + s, z + s * k, other))

    peers = 5 + jnp.where(u <= 2, 1, 0) + jnp.where(u >= HALF - 3, 1, 0) + jnp.where(u == HALF - 1, 3, 0)
    pl.semaphore_wait(barrier, peers)

    def remote(src, dst, send, recv, d):
        return pltpu.make_async_remote_copy(
            src_ref=src, dst_ref=dst, send_sem=send, recv_sem=recv, device_id=d, device_id_type=MESH
        )

    pltpu.make_async_copy(text, own.at[1], local.at[1]).wait()

    def part(ref, slot, q):
        return ref.at[slot, pl.ds(pl.multiple_of(q * piece, piece), piece)]

    def injected(q):
        return remote(part(own, 1, q), part(slots, 0, q), ring_send.at[X0, q], ring_recv.at[0, q], inject)

    def onward(j, q):
        return remote(part(slots, j, q), part(slots, j + 1, q), ring_send.at[j, q], ring_recv.at[j + 1, q], ahead)

    for q in range(PARTS):
        injected(q).start()

    pltpu.make_async_copy(text, own.at[0], local.at[0]).wait()
    to_partner = remote(own.at[0], slots.at[K0], first_send.at[0], near_recv.at[0], partner)
    to_around = remote(own.at[0], slots.at[K0 + 3], first_send.at[1], near_recv.at[3], around)
    to_side = remote(own.at[1], slots.at[X0 + k_side], first_send.at[2], side_recv.at[k_side], side)
    to_partner.start()
    is_around, is_side = u <= 2, u >= HALF - 3
    pl.when(is_around)(to_around.start)
    pl.when(is_side)(to_side.start)

    def near_on(k):
        return remote(slots.at[K0 + k], slots.at[K0 + k + 1], near_send.at[k], near_recv.at[k + 1], ahead)

    def near_back(k):
        return remote(slots.at[K0 + k], slots.at[K0 + k - 1], near_send.at[k], near_recv.at[k - 1], behind)

    def side_back(k):
        return remote(slots.at[X0 + k], slots.at[X0 + k + 1], side_send.at[k], side_recv.at[k + 1], behind)

    def near_arrived(k):
        remote(slots.at[K0 + k], slots.at[K0 + k], near_send.at[k], near_recv.at[k], ahead).wait_recv()

    def goes_on(k):
        return (u >= k) & (u < LAST - 2)

    def takes_blocks(k):
        return (u >= k) & (u < LAST - 1) if k else u >= 0

    def lends(k):
        return (u == 2) | (u == 1) if k == 1 else u == 2

    def lend(k):
        place = jnp.where(u == 2, 1 + k, 3)
        return remote(slots.at[K0 + k], own.at[place], own_send.at[k], own_recv.at[place], partner)

    def sum_on(n):
        return remote(sums.at[n], sums.at[2 + n], sum_send.at[n], sum_recv.at[n], ahead)

    def own_arrived(place):
        remote(own.at[place], own.at[place], own_send.at[1], own_recv.at[place], partner).wait_recv()

    def sum_arrived(n):
        remote(sums.at[2 + n], sums.at[2 + n], sum_send.at[n], sum_recv.at[n], ahead).wait_recv()

    def goes_back(k):
        return (u < k) & (u >= 1)

    def near_plain(k):
        @pl.when(takes_blocks(k))
        def _():
            near_arrived(k)

        if k < 2:
            pl.when(goes_on(k))(near_on(k).start)
        if k in (1, 2):
            pl.when(lends(k))(lend(k).start)

    def near_third():
        pl.when(goes_on(2))(near_on(2).start)

    def near_direct():
        @pl.when(u < 3)
        def _():
            near_arrived(3)

        pl.when(goes_back(3))(near_back(3).start)

    def near_wrapped(k):
        @pl.when(u < k)
        def _():
            near_arrived(k)

        if k == 2:
            pl.when(goes_back(k))(near_back(k).start)

    def side_goes(k):
        return u >= HALF - 3 + (3 - k)

    def side_step(k):
        @pl.when(side_goes(k))
        def _():
            remote(slots.at[X0 + k], slots.at[X0 + k], side_send.at[k], side_recv.at[k], ahead).wait_recv()

        if k < 3:
            pl.when(side_goes(k))(side_back(k).start)

    def ring_step(j):
        for q in range(PARTS):
            remote(part(slots, j, q), part(slots, j, q), ring_send.at[j, q], ring_recv.at[j, q], ahead).wait_recv()
            onward(j, q).start()

    pltpu.make_async_copy(shifts, shift_rows, local.at[2]).wait()
    multiplier, shift = factor[0], bias[0]
    at_blk = lax.broadcasted_iota(jnp.int32, (1, shift_rows.shape[1]), 1) == blk

    def shift_of(slab_index):
        return jnp.sum(jnp.where(at_blk, shift_rows[pl.ds(slab_index, 1), :], 0), axis=1, keepdims=True)

    as_image = shift_of(slab)
    as_caption = rows - shift_of(lax.rem(slab + 1, 16))
    near_offset = jnp.where(core == 0, as_caption, as_image)
    far_offset = jnp.where(core == 0, as_image, as_caption)

    def task(role, k, block, offset, first=0):
        similarity = multiplier * lax.dot_general(
            own[role], block, (((1,), (1,)), ((), ())), preferred_element_type=jnp.float32
        ) + shift
        likely = jax.nn.sigmoid(similarity)
        position = lax.broadcasted_iota(jnp.int32, likely.shape, 0)
        column = lax.broadcasted_iota(jnp.int32, likely.shape, 1) + first
        hit = jnp.where(column == lax.rem(position + offset, rows), 1.0, 0.0)
        likely = likely - hit * jnp.where(k == 0, 1.0, 0.0)
        weight = likely.astype(jnp.bfloat16)
        totals[role] += jnp.dot(weight, block, preferred_element_type=jnp.float32)

    totals[...] = jnp.zeros_like(totals)

    def step(j, carry):
        ring_step(j)

        for first, action in (
            (1, lambda: near_plain(0)),
            (3, lambda: near_plain(1)),
            (4, near_direct),
            (5, lambda: near_plain(2)),
            (6, lambda: side_step(1)),
            (7, lambda: near_wrapped(2)),
            (9, lambda: side_step(2)),
            (10, lambda: near_wrapped(1)),
            (11, lambda: near_plain(3)),
            (12, lambda: side_step(3)),
            (8, near_third),
        ):
            pl.when(j == first)(action)

        @pl.when((u == LAST - 2) & (j >= 5) & (j <= 7))
        def _():
            pl.when(j == 5)(lambda: own_arrived(2))
            pl.when(j == 7)(lambda: own_arrived(3))

            for n in range(2):
                @pl.when((j != 6) | (n == 0))
                def _():
                    task(jnp.where(j == 7, 3, 2), 1, slots[K0 + jnp.where(j == 6, 2, n)], near_offset)

            for n in range(2):
                @pl.when(j == 6 + n)
                def _():
                    sums[n] = totals[2 + n].astype(jnp.bfloat16)
                    sum_on(n).start()

        @pl.when((u == LAST - 1) & (j == 10))
        def _():
            own_arrived(3)
            task(3, 1, slots[K0], near_offset)
            sum_arrived(1)
            sums[1] = (totals[3] + sums[3].astype(jnp.float32)).astype(jnp.bfloat16)
            sum_on(1).start()
            sum_arrived(0)
            totals[0] += sums[2].astype(jnp.float32)

        @pl.when((j == 8) | (((j == 9) | (j == 10) | (j == 11)) & (u < LAST - 1)))
        def _():
            k = jnp.where(j == 11, 3, jnp.where(j == 10, 1, jnp.where(j == 9, 2, 0)))
            task(0, k, slots[K0 + k], near_offset)

        @pl.when((u == LAST) & (j == 13))
        def _():
            sum_arrived(1)
            totals[0] += sums[3].astype(jnp.float32)

        @pl.when((j == 14) & (core == 0))
        def _():
            pltpu.make_async_copy(totals.at[0], text_out, local.at[0]).start()

        @pl.when((j == 14) & (core == 1))
        def _():
            pltpu.make_async_copy(totals.at[0], photo_out, local.at[0]).start()

        @pl.when(j >= X0 - 3)
        def _():
            k = X0 - j
            task(1, k, slots[jnp.where(u + k < HALF, X0 - k, X0 + k)], far_offset)

        return carry

    lax.fori_loop(0, X0, step, 0)
    for q in range(PARTS):
        last = part(slots, X0, q)
        remote(last, last, ring_send.at[X0, q], ring_recv.at[X0, q], ahead).wait_recv()
        task(1, 0, slots[X0, q * piece : (q + 1) * piece], far_offset, q * piece)

    @pl.when(core == 0)
    def _():
        pltpu.make_async_copy(totals.at[1], photo_out, local.at[1]).start()

    @pl.when(core == 1)
    def _():
        pltpu.make_async_copy(totals.at[1], text_out, local.at[1]).start()

    def sent(j, carry):
        for q in range(PARTS):
            onward(j, q).wait_send()
        return carry

    lax.fori_loop(0, X0, sent, 0)
    for q in range(PARTS):
        injected(q).wait_send()
    to_partner.wait_send()
    pl.when(is_around)(to_around.wait_send)
    pl.when(is_side)(to_side.wait_send)
    for k in range(3):
        pl.when(goes_on(k))(near_on(k).wait_send)
    for k in (2, 3):
        pl.when(goes_back(k))(near_back(k).wait_send)
    for k in (1, 2):
        pl.when(side_goes(k))(side_back(k).wait_send)
    for k in (1, 2):
        pl.when(lends(k))(lend(k).wait_send)
    pl.when(u == LAST - 2)(sum_on(0).wait_send)
    pl.when((u == LAST - 2) | (u == LAST - 1))(sum_on(1).wait_send)
    for role in range(2):
        pltpu.make_async_copy(totals.at[role], photo_out, local.at[role]).wait()


def body(photo_features, text_features, partner_displacement, multiplier_factor, additive_shift_term):
    rows, width = photo_features.shape
    anywhere = pl.BlockSpec(memory_space=pl.ANY)
    hbm = pl.BlockSpec(memory_space=pltpu.HBM)
    scalars = pl.BlockSpec(memory_space=pltpu.SMEM)
    total = jax.ShapeDtypeStruct((rows, width), jnp.float32)
    photo, text = pl.pallas_call(
        kernel,
        out_shape=(total, total),
        in_specs=[hbm, hbm, hbm, scalars, scalars],
        out_specs=(anywhere, anywhere),
        scratch_shapes=[
            pltpu.VMEM((4, rows, width), jnp.bfloat16),
            pltpu.VMEM((SLOTS, rows, width), jnp.bfloat16),
            pltpu.VMEM((4, rows, width), jnp.float32),
            pltpu.VMEM((4, rows, width), jnp.bfloat16),
            pltpu.VMEM(partner_displacement.shape[::-1], jnp.int32),
            pltpu.SemaphoreType.DMA((HALF, PARTS)),
            pltpu.SemaphoreType.DMA((HALF, PARTS)),
            pltpu.SemaphoreType.DMA((STEPS,)),
            pltpu.SemaphoreType.DMA((STEPS,)),
            pltpu.SemaphoreType.DMA((STEPS,)),
            pltpu.SemaphoreType.DMA((STEPS,)),
            pltpu.SemaphoreType.DMA((3,)),
            pltpu.SemaphoreType.DMA((STEPS,)),
            pltpu.SemaphoreType.DMA((STEPS,)),
            pltpu.SemaphoreType.DMA((2,)),
            pltpu.SemaphoreType.DMA((2,)),
            pltpu.SemaphoreType.DMA((3,)),
        ],
        compiler_params=pltpu.CompilerParams(
            collective_id=0, has_side_effects=True, vmem_limit_bytes=56 * 2**20
        ),
        cost_estimate=pl.CostEstimate(
            flops=32 * rows * rows * width, bytes_accessed=12 * rows * width, transcendentals=8 * rows * rows
        ),
    )(
        photo_features, text_features, partner_displacement.T,
        multiplier_factor.reshape(1), additive_shift_term.reshape(1),
    )
    return multiplier_factor * photo, multiplier_factor * text


def solution(mesh):
    return jax.shard_map(
        body,
        mesh=mesh,
        in_specs=(P(("blk", "slab"), None), P(("blk", "slab"), None), P(), P(), P()),
        out_specs=(P(("blk", "slab"), None), P(("blk", "slab"), None)),
        check_vma=False,
    )
```

```python
import functools

import jax
import jax.numpy as jnp
from jax import lax
from jax.experimental import pallas as pl
from jax.experimental.pallas import tpu as pltpu
from jax.sharding import PartitionSpec as P

MESH = pl.DeviceIdType.MESH
STEPS = 4
NX, NY, HALF = 4, 4, 16
RING = 2 * HALF
X0 = HALF - 1
K0 = HALF + STEPS - 1
SLOTS = K0 + STEPS
LAST = HALF - 1
PARTS = 8


def device(x, y, z, core):
    x, y, z = (x + NX) % NX, (y + NY) % NY, (z + RING) % RING
    return {"blk": y * HALF + z % HALF, "slab": x * 4 + (z // HALF) * 2 + core}


def kernel(
    photo, text, shifts, factor, bias, photo_out, text_out,
    own, slots, totals, sums, shift_rows, ring_send, ring_recv, near_send, near_recv, side_send, side_recv, first_send,
    own_send, own_recv, sum_send, sum_recv, local,
):
    blk, slab = lax.axis_index("blk"), lax.axis_index("slab")
    x, half, core = slab // 4, (slab // 2) % 2, slab % 2
    y, z_lo = blk // HALF, blk % HALF
    z = half * HALF + z_lo
    other = 1 - core
    s = 2 * core - 1
    u = jnp.where(core == 1, z_lo, HALF - 1 - z_lo)
    rows = own.shape[1]
    piece = rows // PARTS

    pltpu.make_async_copy(shifts, shift_rows, local.at[2]).start()

    @pl.when(core == 0)
    def _():
        pltpu.make_async_copy(text, own.at[0], local.at[0]).start()
        pltpu.make_async_copy(photo, own.at[1], local.at[1]).start()

    @pl.when(core == 1)
    def _():
        pltpu.make_async_copy(photo, own.at[0], local.at[0]).start()
        pltpu.make_async_copy(text, own.at[1], local.at[1]).start()

    ahead = device(x, y, z + s, core)
    behind = device(x, y, z - s, core)
    partner = device(x, y, z, other)
    x_far = jnp.where(core == 0, x - (1 - half), x + half)

    def x_from(z_source):
        h = ((z_source + RING) % RING) // HALF
        return jnp.where(core == 0, x - h, x + (1 - h))

    inject = device(x_far, y, z - s, other)
    inject_from = device(x_from(z - s), y, z - s, other)
    around = device(x, y - s, half * HALF + (z_lo + s * (HALF - 3) + RING) % HALF, other)
    k_side = jnp.minimum(HALF - u, STEPS - 1)
    side = device(x_far, y + s, z + s * k_side, other)

    barrier = pltpu.get_barrier_semaphore()

    def greet(d):
        pl.semaphore_signal(barrier, inc=1, device_id=d, device_id_type=MESH)

    for d in (ahead, behind, partner, inject, inject_from):
        greet(d)

    @pl.when(u <= 2)
    def _():
        greet(around)

    @pl.when(u >= HALF - 3)
    def _():
        greet(side)

    @pl.when(u == HALF - 1)
    def _():
        for k in range(1, STEPS):
            greet(device(x_from(z + s * k), y + s, z + s * k, other))

    peers = 5 + jnp.where(u <= 2, 1, 0) + jnp.where(u >= HALF - 3, 1, 0) + jnp.where(u == HALF - 1, 3, 0)
    pl.semaphore_wait(barrier, peers)

    def remote(src, dst, send, recv, d):
        return pltpu.make_async_remote_copy(
            src_ref=src, dst_ref=dst, send_sem=send, recv_sem=recv, device_id=d, device_id_type=MESH
        )

    pltpu.make_async_copy(text, own.at[1], local.at[1]).wait()

    def part(ref, slot, q):
        return ref.at[slot, pl.ds(pl.multiple_of(q * piece, piece), piece)]

    def injected(q):
        return remote(part(own, 1, q), part(slots, 0, q), ring_send.at[X0, q], ring_recv.at[0, q], inject)

    def onward(j, q):
        return remote(part(slots, j, q), part(slots, j + 1, q), ring_send.at[j, q], ring_recv.at[j + 1, q], ahead)

    for q in range(PARTS):
        injected(q).start()

    pltpu.make_async_copy(text, own.at[0], local.at[0]).wait()
    to_partner = remote(own.at[0], slots.at[K0], first_send.at[0], near_recv.at[0], partner)
    to_around = remote(own.at[0], slots.at[K0 + 3], first_send.at[1], near_recv.at[3], around)
    to_side = remote(own.at[1], slots.at[X0 + k_side], first_send.at[2], side_recv.at[k_side], side)
    to_partner.start()
    is_around, is_side = u <= 2, u >= HALF - 3
    pl.when(is_around)(to_around.start)
    pl.when(is_side)(to_side.start)

    def near_on(k):
        return remote(slots.at[K0 + k], slots.at[K0 + k + 1], near_send.at[k], near_recv.at[k + 1], ahead)

    def near_back(k):
        return remote(slots.at[K0 + k], slots.at[K0 + k - 1], near_send.at[k], near_recv.at[k - 1], behind)

    def side_back(k):
        return remote(slots.at[X0 + k], slots.at[X0 + k + 1], side_send.at[k], side_recv.at[k + 1], behind)

    def near_arrived(k):
        remote(slots.at[K0 + k], slots.at[K0 + k], near_send.at[k], near_recv.at[k], ahead).wait_recv()

    def goes_on(k):
        return (u >= k) & (u < LAST - 2)

    def takes_blocks(k):
        return (u >= k) & (u < LAST - 1) if k else u >= 0

    def lends(k):
        return (u == 2) | (u == 1) if k == 1 else u == 2

    def lend(k):
        place = jnp.where(u == 2, 1 + k, 3)
        return remote(slots.at[K0 + k], own.at[place], own_send.at[k], own_recv.at[place], partner)

    def sum_on(n):
        return remote(sums.at[n], sums.at[2 + n], sum_send.at[n], sum_recv.at[n], ahead)

    def own_arrived(place):
        remote(own.at[place], own.at[place], own_send.at[1], own_recv.at[place], partner).wait_recv()

    def sum_arrived(n):
        remote(sums.at[2 + n], sums.at[2 + n], sum_send.at[n], sum_recv.at[n], ahead).wait_recv()

    def goes_back(k):
        return (u < k) & (u >= 1)

    def near_plain(k):
        @pl.when(takes_blocks(k))
        def _():
            near_arrived(k)

        if k < 2:
            pl.when(goes_on(k))(near_on(k).start)
        if k in (1, 2):
            pl.when(lends(k))(lend(k).start)

    def near_third():
        pl.when(goes_on(2))(near_on(2).start)

    def near_direct():
        @pl.when(u < 3)
        def _():
            near_arrived(3)

        pl.when(goes_back(3))(near_back(3).start)

    def near_wrapped(k):
        @pl.when(u < k)
        def _():
            near_arrived(k)

        if k == 2:
            pl.when(goes_back(k))(near_back(k).start)

    def side_goes(k):
        return u >= HALF - 3 + (3 - k)

    def side_step(k):
        @pl.when(side_goes(k))
        def _():
            remote(slots.at[X0 + k], slots.at[X0 + k], side_send.at[k], side_recv.at[k], ahead).wait_recv()

        if k < 3:
            pl.when(side_goes(k))(side_back(k).start)

    def ring_step(j):
        for q in range(PARTS):
            remote(part(slots, j, q), part(slots, j, q), ring_send.at[j, q], ring_recv.at[j, q], ahead).wait_recv()
            onward(j, q).start()

    pltpu.make_async_copy(shifts, shift_rows, local.at[2]).wait()
    multiplier, shift = factor[0], bias[0]
    at_blk = lax.broadcasted_iota(jnp.int32, (1, shift_rows.shape[1]), 1) == blk

    def shift_of(slab_index):
        return jnp.sum(jnp.where(at_blk, shift_rows[pl.ds(slab_index, 1), :], 0), axis=1, keepdims=True)

    as_image = shift_of(slab)
    as_caption = rows - shift_of(lax.rem(slab + 1, 16))
    near_offset = jnp.where(core == 0, as_caption, as_image)
    far_offset = jnp.where(core == 0, as_image, as_caption)

    def task(role, k, block, offset, first=0):
        similarity = multiplier * lax.dot_general(
            own[role], block, (((1,), (1,)), ((), ())), preferred_element_type=jnp.float32
        ) + shift
        likely = jax.nn.sigmoid(similarity)
        position = lax.broadcasted_iota(jnp.int32, likely.shape, 0)
        column = lax.broadcasted_iota(jnp.int32, likely.shape, 1) + first
        hit = jnp.where(column == lax.rem(position + offset, rows), 1.0, 0.0)
        likely = likely - hit * jnp.where(k == 0, 1.0, 0.0)
        weight = likely.astype(jnp.bfloat16)
        totals[role] += jnp.dot(weight, block, preferred_element_type=jnp.float32)

    totals[...] = jnp.zeros_like(totals)

    def step(j, carry):
        ring_step(j)

        for first, action in (
            (1, lambda: near_plain(0)),
            (3, lambda: near_plain(1)),
            (4, near_direct),
            (5, lambda: near_plain(2)),
            (6, lambda: side_step(1)),
            (7, lambda: near_wrapped(2)),
            (9, lambda: side_step(2)),
            (10, lambda: near_wrapped(1)),
            (11, lambda: near_plain(3)),
            (12, lambda: side_step(3)),
            (8, near_third),
        ):
            pl.when(j == first)(action)

        @pl.when((u == LAST - 2) & (j >= 5) & (j <= 7))
        def _():
            pl.when(j == 5)(lambda: own_arrived(2))
            pl.when(j == 7)(lambda: own_arrived(3))

            for n in range(2):
                @pl.when((j != 6) | (n == 0))
                def _():
                    task(jnp.where(j == 7, 3, 2), 1, slots[K0 + jnp.where(j == 6, 2, n)], near_offset)

            for n in range(2):
                @pl.when(j == 6 + n)
                def _():
                    sums[n] = totals[2 + n].astype(jnp.bfloat16)
                    sum_on(n).start()

        @pl.when((u == LAST - 1) & (j == 10))
        def _():
            own_arrived(3)
            task(3, 1, slots[K0], near_offset)
            sum_arrived(1)
            sums[1] = (totals[3] + sums[3].astype(jnp.float32)).astype(jnp.bfloat16)
            sum_on(1).start()
            sum_arrived(0)
            totals[0] += sums[2].astype(jnp.float32)

        @pl.when((j == 8) | (((j == 9) | (j == 10) | (j == 11)) & (u < LAST - 1)))
        def _():
            k = jnp.where(j == 11, 3, jnp.where(j == 10, 1, jnp.where(j == 9, 2, 0)))
            task(0, k, slots[K0 + k], near_offset)

        @pl.when((u == LAST) & (j == 13))
        def _():
            sum_arrived(1)
            totals[0] += sums[3].astype(jnp.float32)

        @pl.when((j == 14) & (core == 0))
        def _():
            pltpu.make_async_copy(totals.at[0], text_out, local.at[0]).start()

        @pl.when((j == 14) & (core == 1))
        def _():
            pltpu.make_async_copy(totals.at[0], photo_out, local.at[0]).start()

        @pl.when(j >= X0 - 3)
        def _():
            k = X0 - j
            task(1, k, slots[jnp.where(u + k < HALF, X0 - k, X0 + k)], far_offset)

        return carry

    lax.fori_loop(0, X0, step, 0)
    for q in range(PARTS):
        last = part(slots, X0, q)
        remote(last, last, ring_send.at[X0, q], ring_recv.at[X0, q], ahead).wait_recv()
        task(1, 0, slots[X0, q * piece : (q + 1) * piece], far_offset, q * piece)

    @pl.when(core == 0)
    def _():
        pltpu.make_async_copy(totals.at[1], photo_out, local.at[1]).start()

    @pl.when(core == 1)
    def _():
        pltpu.make_async_copy(totals.at[1], text_out, local.at[1]).start()

    def sent(j, carry):
        for q in range(PARTS):
            onward(j, q).wait_send()
        return carry

    lax.fori_loop(0, X0, sent, 0)
    for q in range(PARTS):
        injected(q).wait_send()
    to_partner.wait_send()
    pl.when(is_around)(to_around.wait_send)
    pl.when(is_side)(to_side.wait_send)
    for k in range(3):
        pl.when(goes_on(k))(near_on(k).wait_send)
    for k in (2, 3):
        pl.when(goes_back(k))(near_back(k).wait_send)
    for k in (1, 2):
        pl.when(side_goes(k))(side_back(k).wait_send)
    for k in (1, 2):
        pl.when(lends(k))(lend(k).wait_send)
    pl.when(u == LAST - 2)(sum_on(0).wait_send)
    pl.when((u == LAST - 2) | (u == LAST - 1))(sum_on(1).wait_send)
    for role in range(2):
        pltpu.make_async_copy(totals.at[role], photo_out, local.at[role]).wait()


def body(photo_features, text_features, partner_displacement, multiplier_factor, additive_shift_term):
    rows, width = photo_features.shape
    anywhere = pl.BlockSpec(memory_space=pl.ANY)
    hbm = pl.BlockSpec(memory_space=pltpu.HBM)
    scalars = pl.BlockSpec(memory_space=pltpu.SMEM)
    total = jax.ShapeDtypeStruct((rows, width), jnp.float32)
    photo, text = pl.pallas_call(
        kernel,
        out_shape=(total, total),
        in_specs=[hbm, hbm, hbm, scalars, scalars],
        out_specs=(anywhere, anywhere),
        scratch_shapes=[
            pltpu.VMEM((4, rows, width), jnp.bfloat16),
            pltpu.VMEM((SLOTS, rows, width), jnp.bfloat16),
            pltpu.VMEM((4, rows, width), jnp.float32),
            pltpu.VMEM((4, rows, width), jnp.bfloat16),
            pltpu.VMEM(partner_displacement.shape[::-1], jnp.int32),
            pltpu.SemaphoreType.DMA((HALF, PARTS)),
            pltpu.SemaphoreType.DMA((HALF, PARTS)),
            pltpu.SemaphoreType.DMA((STEPS,)),
            pltpu.SemaphoreType.DMA((STEPS,)),
            pltpu.SemaphoreType.DMA((STEPS,)),
            pltpu.SemaphoreType.DMA((STEPS,)),
            pltpu.SemaphoreType.DMA((3,)),
            pltpu.SemaphoreType.DMA((STEPS,)),
            pltpu.SemaphoreType.DMA((STEPS,)),
            pltpu.SemaphoreType.DMA((2,)),
            pltpu.SemaphoreType.DMA((2,)),
            pltpu.SemaphoreType.DMA((3,)),
        ],
        compiler_params=pltpu.CompilerParams(
            collective_id=0, has_side_effects=True, vmem_limit_bytes=56 * 2**20
        ),
        cost_estimate=pl.CostEstimate(
            flops=32 * rows * rows * width, bytes_accessed=12 * rows * width, transcendentals=8 * rows * rows
        ),
    )(
        photo_features, text_features, partner_displacement.T,
        multiplier_factor.reshape(1), additive_shift_term.reshape(1),
    )
    return multiplier_factor * photo, multiplier_factor * text


def solution(mesh):
    return jax.shard_map(
        body,
        mesh=mesh,
        in_specs=(P(("blk", "slab"), None), P(("blk", "slab"), None), P(), P(), P()),
        out_specs=(P(("blk", "slab"), None), P(("blk", "slab"), None)),
        check_vma=False,
    )
```
